32 devices in a mesh: tm: 4 (over z), space: 8 (over y, x, core).
Axes of the slice: x: 2, y: 2, z: 4, core: 2. Of those that a mesh axis runs over, the one named last changes fastest.
Arguments:
- height_residual: float32 [32, 128, 2048], P('tm', 'space'), may hold values from -6 to 6
- east_residual: float32 [32, 128, 2048], P('tm', 'space'), may hold values from -6 to 6
- north_residual: float32 [32, 128, 2048], P('tm', 'space'), may hold values from -6 to 6
Outputs:
- height_update: float32 [32, 128, 2048], P('tm', 'space')
- east_update: float32 [32, 128, 2048], P('tm', 'space')
- north_update: float32 [32, 128, 2048], P('tm', 'space')
The draws below stay inside these ranges and needn't reach their ends.
All inputs are finite; a program needn't handle non-finite values.
Results may differ from the reference program's by a relative error of at most 0.00019.
Values sent between devices are 32-bit elements; how exact they have to be, the bound alone decides.
No kernel may reach another device: no remote copies, remote signals or barrier semaphores. Data moves between devices by JAX's collectives and lax.ppermute only.
A program may use at most 128 MiB of HBM per device.

```python
import math
import jax
import jax.numpy as jnp
from jax import lax

NX = 2048
STEPS = 32
NY = 128


def level_of(key, extent, cuts, least, high):
    gain, own = 1.0, jax.random.fold_in(key, 6)
    for dim, blocks in cuts:
        steps = jnp.exp(jax.random.uniform(jax.random.fold_in(own, dim), (blocks,), jnp.float32, least / len(cuts), high / len(cuts)))
        gain = gain * jnp.repeat(steps, extent[dim] // blocks).reshape([-1 if axis == dim else 1 for axis in range(len(extent))])
    return gain


def noise(rng, shape, spread, most, split=(), dtype=jnp.bfloat16):
    factor_of = level_of(rng, shape, split, -0.22, 0.18) if split else 1.0
    result = jax.random.normal(rng, shape, jnp.float32) * spread * factor_of
    return jnp.minimum(jnp.maximum(result, -most), most).astype(dtype)


def setup_inputs(seed: int = 0) -> dict:
    seeds = jax.random.split(jax.random.key(seed), 4)
    return {
        "height_residual": noise(seeds[0], (STEPS, NY, NX), 1.0, 6.0, ((0, 4), (1, 8)), jnp.float32),
        "east_residual": noise(seeds[1], (STEPS, NY, NX), 1.0, 6.0, ((0, 4), (1, 8)), jnp.float32),
        "north_residual": noise(seeds[2], (STEPS, NY, NX), 1.0, 6.0, ((0, 4), (1, 8)), jnp.float32),
    }


alpha_window = 0.1
gravity = 1.0
mean_depth = 0.25
coriolis = 0.3
wave_speed = gravity * mean_depth


def complex_product(first, second):
    return (first[0] * second[0] - first[1] * second[1], first[0] * second[1] + first[1] * second[0])


def frequency_terms(freqs, steps):
    root_rate = alpha_window ** (1.0 / steps)
    angles = freqs * (2.0 * math.pi / steps)
    spectral_shift = (1.0 - root_rate * jnp.cos(angles), root_rate * jnp.sin(angles))
    square = (spectral_shift[0] * spectral_shift[0] - spectral_shift[1] * spectral_shift[1] + coriolis * coriolis,
              2.0 * spectral_shift[0] * spectral_shift[1])
    shift_norm = spectral_shift[0] * spectral_shift[0] + spectral_shift[1] * spectral_shift[1]
    inv_shift = (spectral_shift[0] / shift_norm, -spectral_shift[1] / shift_norm)
    square_over_shift = complex_product(square, inv_shift)
    turn_over_shift = (coriolis * inv_shift[0], coriolis * inv_shift[1])
    diagonal = (square[0] + 4.0 * wave_speed, square[1])
    diag_norm = diagonal[0] * diagonal[0] + diagonal[1] * diagonal[1]
    inv_diagonal = (diagonal[0] / diag_norm, -diagonal[1] / diag_norm)
    square_norm = square[0] * square[0] + square[1] * square[1]
    inv_square = (square[0] / square_norm, -square[1] / square_norm)
    shift_over_square = complex_product(spectral_shift, inv_square)
    turn_over_square = (coriolis * inv_square[0], coriolis * inv_square[1])
    return (square_over_shift, turn_over_shift, inv_diagonal, shift_over_square, turn_over_square)


def east_diff(values):
    return 0.5 * (jnp.roll(values, -1, -1) - jnp.roll(values, 1, -1))


def north_diff(values):
    return 0.5 * (values[..., 2:, :] - values[..., :-2, :])


def trim_rows(values, margin):
    return values[..., margin:values.shape[-2] - margin, :]


def trim_pair(pair, margin):
    return (trim_rows(pair[0], margin), trim_rows(pair[1], margin))


def neighbours(values):
    return values[..., 2:, :] + values[..., :-2, :] + trim_rows(jnp.roll(values, -1, -1) + jnp.roll(values, 1, -1), 1)


def helmholtz_source(height, east, north, terms):
    divergence = (trim_rows(east_diff(east[0]), 1) + north_diff(north[0]),
                  trim_rows(east_diff(east[1]), 1) + north_diff(north[1]))
    vorticity = (trim_rows(east_diff(north[0]), 1) - north_diff(east[0]),
                 trim_rows(east_diff(north[1]), 1) - north_diff(east[1]))
    turned = complex_product(terms[1], vorticity)
    scaled = complex_product(terms[0], height)
    return (scaled[0] - mean_depth * (divergence[0] + turned[0]),
            scaled[1] - mean_depth * (divergence[1] + turned[1]))


def jacobi_sweep(height, source, inv_diagonal):
    total = (source[0] + wave_speed * neighbours(height[0]), source[1] + wave_speed * neighbours(height[1]))
    return complex_product(total, inv_diagonal)


def velocities(height, east, north, terms):
    east_force = (east[0] - gravity * east_diff(trim_rows(height[0], 1)),
                  east[1] - gravity * east_diff(trim_rows(height[1], 1)))
    north_force = (north[0] - gravity * north_diff(height[0]), north[1] - gravity * north_diff(height[1]))
    first = complex_product(terms[3], east_force)
    second = complex_product(terms[4], north_force)
    third = complex_product(terms[3], north_force)
    fourth = complex_product(terms[4], east_force)
    return (first[0] + second[0], first[1] + second[1]), (third[0] - fourth[0], third[1] - fourth[1])


def wrap_pair(pair):
    return (jnp.concatenate([pair[0][-1:], pair[0], pair[0][:1]], axis=0),
            jnp.concatenate([pair[1][-1:], pair[1], pair[1][:1]], axis=0))


def solve_frequency(inputs):
    freq_value, height_re, height_im, east_re, east_im, north_re, north_im = inputs
    terms = frequency_terms(freq_value, STEPS)
    east = wrap_pair((east_re, east_im))
    north = wrap_pair((north_re, north_im))
    source = helmholtz_source((height_re, height_im), east, north, terms)
    height = complex_product(source, terms[2])
    for sweep_count in range(2):
        height = jacobi_sweep(wrap_pair(height), source, terms[2])
    east_out, north_out = velocities(wrap_pair(height), trim_pair(east, 1), trim_pair(north, 1), terms)
    return (height[0], height[1], east_out[0], east_out[1], north_out[0], north_out[1])


def reference(height_residual, east_residual, north_residual):
    log_rate = math.log(alpha_window) / STEPS
    step_ids = jnp.arange(STEPS).astype(jnp.float32)
    weights = jnp.exp(step_ids * log_rate)[:, None, None]
    spectra = []
    for residual in (height_residual, east_residual, north_residual):
        spectrum = jnp.fft.fft(residual * weights, axis=0)
        spectra = spectra + [jnp.real(spectrum), jnp.imag(spectrum)]
    solved = lax.map(solve_frequency, (step_ids,) + tuple(spectra))
    unweights = jnp.exp(-step_ids * log_rate)[:, None, None]
    outputs = []
    for member in range(3):
        inverse = jnp.fft.ifft(lax.complex(solved[2 * member], solved[2 * member + 1]), axis=0)
        outputs.append(jnp.real(inverse) * unweights)
    return (outputs[0], outputs[1], outputs[2])
```

```python
import functools
import math

import jax
import jax.numpy as jnp
import numpy as np
from jax import lax
from jax.experimental import pallas as pl
from jax.experimental.pallas import tpu as pltpu
from jax.sharding import PartitionSpec as P

alpha_window = 0.1
gravity = 1.0
mean_depth = 0.25
coriolis = 0.3
wave_speed = gravity * mean_depth
diagonal = 1.0 + coriolis * coriolis + 4.0 * wave_speed
turn_norm = 1.0 / (1.0 + coriolis * coriolis)
LANES = 128
MIB = 1 << 20

WIDTH = (1, 3, 3, 5, 5, 7, 7)
ENTRIES = [(i, j) for i in range(7) for j in range(WIDTH[i])]


def step_matrix():
    m = np.zeros((7, 7))
    m[0, 0] = 1.0
    source = np.zeros(7)
    source[0] = coriolis
    for k in range(3):
        u, r = 1 + 2 * k, 2 + 2 * k
        new = source.copy()
        new[u] += 1.0
        new = new / diagonal
        m[r] = new
        m[u] = 2.0 * new
        m[u, r] -= 1.0
        source = wave_speed * new
    return m


def tables(parts, steps_local):
    one = step_matrix()
    turn = 1.0 / (1.0 + 1j * coriolis)
    block = np.linalg.matrix_power(one, steps_local)
    spin = turn**steps_local
    power = lambda k: np.linalg.matrix_power(block, k)
    closure = np.linalg.inv(np.eye(7) - alpha_window * power(parts))
    closure_spin = 1.0 / (1.0 - alpha_window * spin**parts)
    zero, eye = np.zeros((7, 7)), np.eye(7)
    fields, turns = [], []
    for b in range(parts):
        row, spins = [], []
        row.append(alpha_window * closure @ power(parts - 1))
        spins.append(alpha_window * closure_spin * spin ** (parts - 1))
        for hop in range(1, parts):
            if hop == b:
                row.append(closure)
                spins.append(closure_spin)
            elif hop == parts - 1 - b:
                row.append(alpha_window * closure @ power(b))
                spins.append(alpha_window * closure_spin * spin**b)
            else:
                row.append(zero)
                spins.append(0.0)
            following = hop + 1
            if b == following - 1:
                row += [block, eye]
                spins += [spin, 1.0]
            elif b == parts - following:
                row += [eye, power(parts - 1 - b)]
                spins += [1.0, spin ** (parts - 1 - b)]
            else:
                row += [zero, zero]
                spins += [0.0, 0.0]
        fields.append(np.concatenate([[m[i, j] for i, j in ENTRIES] for m in row]))
        turns.append(np.concatenate([[np.real(s), np.imag(s)] for s in spins]))
    return np.concatenate([np.array(fields), np.array(turns)], axis=1).astype(np.float32)


def start_rows():
    one = step_matrix()
    inverse = np.linalg.inv((1.0 + 1j * coriolis) * one - np.eye(7))
    return [one[2 + 2 * k] @ inverse for k in range(3)]


def low_half(shape):
    return lax.broadcasted_iota(jnp.int32, shape, len(shape) - 2) < 4


def wide(load, start, width, total):
    left = pl.multiple_of(lax.rem(start + (total - LANES), total), LANES)
    right = pl.multiple_of(lax.rem(start + width, total), LANES)
    return jnp.concatenate(
        [load(pl.ds(left, LANES)), load(pl.ds(start, width)), load(pl.ds(right, LANES))], axis=-1
    )


def core(x):
    return x[:, LANES : x.shape[1] - LANES]


def next_column(x):
    return core(pltpu.roll(x, x.shape[1] - 1, 1))


def previous_column(x):
    return core(pltpu.roll(x, 1, 1))


def next_row(x):
    return pltpu.roll(x, x.shape[0] - 1, 0)


def previous_row(x):
    return pltpu.roll(x, 1, 0)


def dx(x):
    return 0.5 * (next_column(x) - previous_column(x))


def dy(x):
    return 0.5 * (next_row(x) - previous_row(x))


def neighbours(x):
    middle = core(x)
    return (next_row(middle) + previous_row(middle)) + (next_column(x) + previous_column(x))


def turn_kernel(e_ref, n_ref, out_ref, *, width):
    steps, _, total = e_ref.shape

    def block(i, carry):
        cols = pl.ds(pl.multiple_of(i * width, width), width)
        re, im = e_ref[0, :, cols], n_ref[0, :, cols]
        re, im = turn_norm * (re + coriolis * im), turn_norm * (im - coriolis * re)
        for step in range(1, steps):
            re, im = re + e_ref[step, :, cols], im + n_ref[step, :, cols]
            re, im = turn_norm * (re + coriolis * im), turn_norm * (im - coriolis * re)
        out_ref[0, :, cols] = re
        out_ref[1, :, cols] = im
        return carry

    lax.fori_loop(0, total // width, block, 0)


def source_kernel(
    h_ref, e_ref, n_ref, before_ref, after_ref, src_ref, edge_ref, inner_ref, prev_ref, next_ref, *, width
):
    steps, rows, total = h_ref.shape

    def block(i, carry):
        start = pl.multiple_of(i * width, width)
        cols = pl.ds(start, width)
        row = lax.broadcasted_iota(jnp.int32, (rows, width), 0)
        first, last = row == 0, row == rows - 1
        low = low_half((8, width))

        def slopes(ref, step, at):
            x = wide(lambda c: ref[step, :, c], start, width, total)
            mid = core(x)
            line = pl.ds(at + step, 1)
            up = jnp.where(last, after_ref[line, cols], next_row(mid))
            down = jnp.where(first, before_ref[line, cols], previous_row(mid))
            return dx(x), 0.5 * (up - down)

        p = jnp.zeros((rows, width), jnp.float32)
        state = [p] * 6
        held = None
        h_last = None
        for step in range(steps):
            h = h_ref[step, :, cols]
            e_x, e_y = slopes(e_ref, step, 0)
            n_x, n_y = slopes(n_ref, step, steps)
            p = p + (coriolis * h - mean_depth * (n_x - e_y))
            change = h if h_last is None else h - h_last
            src = (change - mean_depth * (e_x + n_y)) + coriolis * p
            h_last = h
            src_ref[step, :, cols] = src
            top, bottom = src[:8], src[8:]
            if step % 2 == 0:
                held = (top, bottom)
            else:
                prev_ref[step // 2, :, cols] = jnp.where(low, held[0], pltpu.roll(top, 4, 0))
                next_ref[step // 2, :, cols] = jnp.where(low, pltpu.roll(bottom, 4, 0), held[1])
            state = advance(src, state)
        state[0] = state[0] - h_last
        for k, value in enumerate([p] + state):
            top, bottom = value[:8], value[8:]
            edge_ref[k, :, cols] = jnp.where(low, top, bottom)
            inner_ref[k, :, cols] = jnp.where(low, bottom, top)
        return carry

    lax.fori_loop(0, total // width, block, 0)


def advance(source, state):
    out, x = [], source
    for k in range(3):
        u, r = state[2 * k], state[2 * k + 1]
        new = (x + u) * (1.0 / diagonal)
        out += [2.0 * new - r, new]
        x = wave_speed * new
    return out


def apply_matrix(coef_ref, at, fields):
    out, pos = [], at
    for i in range(7):
        total = None
        for j in range(WIDTH[i]):
            term = coef_ref[pos] * fields[j]
            total = term if total is None else total + term
            pos += 1
        out.append(total)
    return out


def apply_turn(coef_ref, at, fields):
    c, s = coef_ref[at], coef_ref[at + 1]
    return [c * fields[0] - s * fields[1], c * fields[1] + s * fields[0]]


def combine_kernel(coef_ref, *refs, hop, parts, apply, base, size, width):
    refs = list(refs)
    got_ref, own_ref = refs[0], refs[1]
    acc_ref = refs[2] if hop > 1 else None
    outs = refs[3:] if hop > 1 else refs[2:]
    count, _, total = own_ref.shape
    at = base + size * (1 + 3 * (hop - 1))

    def block(i, carry):
        cols = pl.ds(pl.multiple_of(i * width, width), width)
        got = [got_ref[k, :, cols] for k in range(count)]
        part = apply(coef_ref, at, got)
        own = None
        if hop == 1 or hop < parts - 1:
            own = [own_ref[k, :, cols] for k in range(count)]
        if hop == 1:
            base_part = apply(coef_ref, base, own)
        else:
            base_part = [acc_ref[k, :, cols] for k in range(count)]
        for k in range(count):
            outs[0][k, :, cols] = base_part[k] + part[k]
        if hop < parts - 1:
            moved = apply(coef_ref, at + size, got)
            added = apply(coef_ref, at + 2 * size, own)
            for k in range(count):
                outs[1][k, :, cols] = moved[k] + added[k]
        return carry

    lax.fori_loop(0, total // width, block, 0)


def pack_kernel(edge_ref, phi_ref, prev_ref, next_ref, *, width):
    total = edge_ref.shape[2]

    def block(i, carry):
        cols = pl.ds(pl.multiple_of(i * width, width), width)
        low = low_half((8, width))
        tops = [edge_ref[k, :, cols] for k in range(7)] + [phi_ref[k, :8, cols] for k in range(2)]
        bottoms = tops[:7] + [phi_ref[k, 8:, cols] for k in range(2)]
        for t in range(5):
            a, b = 2 * t, min(2 * t + 1, 8)
            prev_ref[t, :, cols] = jnp.where(low, tops[a], pltpu.roll(tops[b], 4, 0))
            next_ref[t, :, cols] = jnp.where(low, pltpu.roll(bottoms[b], 4, 0), bottoms[a])
        return carry

    lax.fori_loop(0, total // width, block, 0)


def unpack(from_next, from_prev, odd, low):
    if odd:
        return pltpu.roll(jnp.where(low, from_prev, from_next), 4, 0)
    return jnp.where(low, from_next, from_prev)


def final_kernel(
    edge_ref, inner_ref, phi_ref, s_after_ref, s_before_ref, src_ref, src_after_ref, src_before_ref,
    e_hbm, n_hbm, h_out, e_out, n_out, r1, r2, r3, ring, e_ref, n_ref, u_ref, v_ref, sems, *, width
):
    steps, rows, total = src_ref.shape
    copies_in = [
        pltpu.make_async_copy(e_hbm, e_ref, sems.at[0]),
        pltpu.make_async_copy(n_hbm, n_ref, sems.at[1]),
    ]
    for copy in copies_in:
        copy.start()
    lines = [np.asarray(line) for line in start_rows()]

    def filters(i, carry):
        cols = pl.ds(pl.multiple_of(i * width, width), width)
        low = low_half((8, width))
        fields = []
        for k in range(9):
            halo = unpack(s_after_ref[k // 2, :, cols], s_before_ref[k // 2, :, cols], k % 2 == 1, low)
            if k < 7:
                edge, inner = edge_ref[k, :, cols], inner_ref[k, :, cols]
                fields.append(
                    jnp.concatenate([jnp.where(low, edge, inner), jnp.where(low, inner, edge), halo], 0)
                )
            else:
                ring[k - 7, :, cols] = jnp.concatenate([phi_ref[k - 7, :, cols], halo], 0)
        for planes, line in ((r1, lines[0]), (r2, lines[1]), (r3, lines[2])):
            for part, weights in ((0, np.real(line)), (1, np.imag(line))):
                value = None
                for j in range(7):
                    if weights[j] != 0.0:
                        term = float(weights[j]) * fields[j]
                        value = term if value is None else value + term
                planes[steps + part, :, cols] = value
        turned = coriolis * fields[0]
        state = fields[1:]
        for step in range(steps):
            pair = step // 2
            halo = unpack(src_after_ref[pair, :, cols], src_before_ref[pair, :, cols], step % 2 == 1, low)
            source = jnp.concatenate([src_ref[step, :, cols], halo], 0) + turned
            state = advance(source, state)
            r1[step, :, cols] = state[1]
            r2[step, :, cols] = state[3]
            r3[step, :, cols] = state[5]
        return carry

    lax.fori_loop(0, total // width, filters, 0)

    def over_blocks(body):
        def at(i, carry):
            start = pl.multiple_of(i * width, width)
            body(start, pl.ds(start, width))
            return carry

        lax.fori_loop(0, total // width, at, 0)

    def spin_terms(start, cols):
        re = wide(lambda c: ring[0, :, c], start, width, total)
        im = wide(lambda c: ring[1, :, c], start, width, total)
        chi = (dx(re) + dy(core(im)), dx(im) - dy(core(re)))
        share = mean_depth / (4.0 * wave_speed)
        for part in range(2):
            r1[steps + part, :, cols] = r1[steps + part, :, cols] - share * chi[part]
            r2[steps + part, :, cols] = r2[steps + part, :, cols] - (share / 4.0) * chi[part]
            r3[steps + part, :, cols] = r3[steps + part, :, cols] - (share / 16.0) * chi[part]

    over_blocks(spin_terms)

    def horner(low_ref, high_ref):
        def body(start, cols):
            def plane(k, carry):
                x = wide(lambda c: high_ref[k, :, c], start, width, total)
                low_ref[k, :, cols] = low_ref[k, :, cols] + neighbours(x)
                return carry

            lax.fori_loop(0, steps + 2, plane, 0)

        over_blocks(body)

    horner(r2, r3)
    horner(r1, r2)
    height_copy = pltpu.make_async_copy(r1.at[pl.ds(0, steps), pl.ds(0, rows)], h_out, sems.at[2])
    height_copy.start()
    for copy in copies_in:
        copy.wait()

    def velocity(start, cols):
        def slopes(k):
            x = wide(lambda c: r1[k, :, c], start, width, total)
            return dx(x)[:rows], dy(core(x))[:rows]

        re_x, re_y = slopes(steps)
        im_x, im_y = slopes(steps + 1)
        u = ring[0, :rows, cols] - gravity * (re_x - im_y)
        v = ring[1, :rows, cols] - gravity * (im_x + re_y)
        for step in range(steps):
            eta_x, eta_y = slopes(step)
            re = u + (e_ref[step, :, cols] - gravity * eta_x)
            im = v + (n_ref[step, :, cols] - gravity * eta_y)
            u, v = turn_norm * (re + coriolis * im), turn_norm * (im - coriolis * re)
            u_ref[step, :, cols] = u
            v_ref[step, :, cols] = v

    over_blocks(velocity)
    copies_out = [
        pltpu.make_async_copy(u_ref, e_out, sems.at[3]),
        pltpu.make_async_copy(v_ref, n_out, sems.at[4]),
    ]
    for copy in copies_out:
        copy.start()
    for copy in copies_out:
        copy.wait()
    height_copy.wait()


VMEM = pl.BlockSpec(memory_space=pltpu.VMEM)
SMEM = pl.BlockSpec(memory_space=pltpu.SMEM)
ANY = pl.BlockSpec(memory_space=pl.ANY)


def f32(*shape):
    return jax.ShapeDtypeStruct(shape, jnp.float32)


def call(kernel, args, outs, in_specs=None, name=None, limit=24, scratch=(), out_specs=None):
    return pl.pallas_call(
        kernel,
        out_shape=outs,
        in_specs=in_specs or [VMEM] * len(args),
        out_specs=out_specs or [VMEM] * len(outs),
        scratch_shapes=scratch,
        compiler_params=pltpu.CompilerParams(vmem_limit_bytes=limit * MIB),
        name=name,
    )(*args)


def shifts(axis):
    count = lax.axis_size(axis)
    forward = [(i, (i + 1) % count) for i in range(count)]
    return forward, [(t, s) for s, t in forward]


def body(h, e, n):
    steps, rows, total = h.shape
    parts = lax.axis_size("tm")
    width = 512 if total % 512 == 0 else LANES
    coef = jnp.asarray(tables(parts, steps))[lax.axis_index("tm")]
    turn_base = len(ENTRIES) * (1 + 3 * (parts - 1))
    forward, backward = shifts("space")

    before = lax.ppermute(jnp.concatenate([e[:, rows - 1], n[:, rows - 1]], 0), "space", forward)
    after = lax.ppermute(jnp.concatenate([e[:, 0], n[:, 0]], 0), "space", backward)

    def hop(x, k):
        return lax.ppermute(x, "tm", [(k - 1, k), (parts - k, parts - 1 - k)])

    def combine(k, got, own, acc, kind):
        apply, base, size = {
            "fields": (apply_matrix, 0, len(ENTRIES)),
            "turn": (apply_turn, turn_base, 2),
        }[kind]
        args = [coef, got, own] + ([acc] if k > 1 else [])
        outs = [f32(*own.shape)] * (2 if k < parts - 1 else 1)
        kernel = functools.partial(
            combine_kernel, hop=k, parts=parts, apply=apply, base=base, size=size,
            width=min(width, own.shape[2]),
        )
        return call(kernel, args, outs, [SMEM] + [VMEM] * (len(args) - 1), f"combine_{kind}_{k}")

    phi = call(functools.partial(turn_kernel, width=width), [e, n], [f32(2, rows, total)], name="turn")[0]
    tile = f32(7, 8, total)
    src, edge, inner, src_prev, src_next = call(
        functools.partial(source_kernel, width=width),
        [h, e, n, before, after],
        [f32(steps, rows, total), tile, tile, f32(steps // 2, 8, total), f32(steps // 2, 8, total)],
        name="source",
    )
    src_after = lax.ppermute(src_prev, "space", backward)
    src_before = lax.ppermute(src_next, "space", forward)

    chunks = [("turn", phi), ("fields", edge), ("fields", inner)]
    message = [c[1] for c in chunks]
    acc = [None] * len(chunks)
    for k in range(1, parts):
        for j, (kind, own) in enumerate(chunks):
            out = combine(k, hop(message[j], k), own, acc[j], kind)
            acc[j] = out[0]
            message[j] = out[1] if k < parts - 1 else None
    phi_in, edge_in, inner_in = acc

    to_prev, to_next = call(
        functools.partial(pack_kernel, width=width), [edge_in, phi_in], [f32(5, 8, total)] * 2, name="pack"
    )
    s_after = lax.ppermute(to_prev, "space", backward)
    s_before = lax.ppermute(to_next, "space", forward)

    planes = pltpu.VMEM((steps + 2, rows + 8, total), jnp.float32)
    whole = pltpu.VMEM((steps, rows, total), jnp.float32)
    return tuple(
        call(
            functools.partial(final_kernel, width=width),
            [edge_in, inner_in, phi_in, s_after, s_before, src, src_after, src_before, e, n],
            [f32(steps, rows, total)] * 3,
            [VMEM] * 8 + [ANY] * 2,
            "final",
            32,
            [planes, planes, planes, pltpu.VMEM((2, rows + 8, total), jnp.float32)]
            + [whole] * 4
            + [pltpu.SemaphoreType.DMA((5,))],
            [ANY] * 3,
        )
    )


def solution(mesh):
    specs = (P("tm", "space", None),) * 3
    return jax.shard_map(body, mesh=mesh, in_specs=specs, out_specs=specs, check_vma=False)
```

```python
import functools
import math

import jax
import jax.numpy as jnp
import numpy as np
from jax import lax
from jax.experimental import pallas as pl
from jax.experimental.pallas import tpu as pltpu
from jax.sharding import PartitionSpec as P

alpha_window = 0.1
gravity = 1.0
mean_depth = 0.25
coriolis = 0.3
wave_speed = gravity * mean_depth
diagonal = 1.0 + coriolis * coriolis + 4.0 * wave_speed
turn_norm = 1.0 / (1.0 + coriolis * coriolis)
LANES = 128
MIB = 1 << 20


def step_matrix():
    m = np.zeros((7, 7))
    m[0, 0] = 1.0
    source = np.zeros(7)
    source[0] = coriolis
    for k in range(3):
        u, r = 1 + 2 * k, 2 + 2 * k
        new = source.copy()
        new[u] += 1.0
        new = new / diagonal
        m[r] = new
        m[u] = 2.0 * new
        m[u, r] -= 1.0
        source = wave_speed * new
    return m


def turn_matrix(value):
    return np.array([[np.real(value), -np.imag(value)], [np.imag(value), np.real(value)]])


def transitions(steps_local):
    spin = (1.0 / (1.0 + 1j * coriolis)) ** steps_local
    return np.linalg.matrix_power(step_matrix(), steps_local), turn_matrix(spin)


def message_weights(block, parts, hop):
    eye, power = np.eye(len(block)), np.linalg.matrix_power
    weights = [None] * parts
    weights[hop] = [block, eye]
    weights[parts - 1 - hop] = [eye, power(block, hop)]
    return weights


def arrival_weight(block, parts, b, hop):
    power = np.linalg.matrix_power
    closure = np.linalg.inv(np.eye(len(block)) - alpha_window * power(block, parts))
    if hop == 0:
        return alpha_window * closure @ power(block, parts - 1)
    if hop == b:
        return closure
    if hop == parts - 1 - b:
        return alpha_window * closure @ power(block, b)
    return None


def start_rows():
    one = step_matrix()
    inverse = np.linalg.inv((1.0 + 1j * coriolis) * one - np.eye(7))
    return [one[2 + 2 * k] @ inverse for k in range(3)]


def low_half(shape):
    return lax.broadcasted_iota(jnp.int32, shape, len(shape) - 2) < 4


def wide(load, start, width, total):
    left = pl.multiple_of(lax.rem(start + (total - LANES), total), LANES)
    right = pl.multiple_of(lax.rem(start + width, total), LANES)
    return jnp.concatenate(
        [load(pl.ds(left, LANES)), load(pl.ds(start, width)), load(pl.ds(right, LANES))], axis=-1
    )


def core(x):
    return x[:, LANES : x.shape[1] - LANES]


def next_column(x):
    return core(pltpu.roll(x, x.shape[1] - 1, 1))


def previous_column(x):
    return core(pltpu.roll(x, 1, 1))


def next_row(x):
    return pltpu.roll(x, x.shape[0] - 1, 0)


def previous_row(x):
    return pltpu.roll(x, 1, 0)


def dx(x):
    return 0.5 * (next_column(x) - previous_column(x))


def dy(x):
    return 0.5 * (next_row(x) - previous_row(x))


def turn_kernel(e_hbm, n_hbm, out_ref, prev_ref, next_ref, e_ref, n_ref, sems, *, width):
    steps, rows, total = e_ref.shape
    copies = []
    for step in range(0, steps, 2):
        part = pl.ds(step, 2)
        copies.append(pltpu.make_async_copy(e_hbm.at[part], e_ref.at[part], sems.at[step]))
        copies.append(pltpu.make_async_copy(n_hbm.at[part], n_ref.at[part], sems.at[step + 1]))
    for copy in copies:
        copy.start()
    for copy in copies:
        copy.wait()
    for step in range(steps):
        for ref, at in ((e_ref, step), (n_ref, steps + step)):
            prev_ref[at : at + 1, :] = ref[step, 0:1, :]
            next_ref[at : at + 1, :] = ref[step, rows - 1 : rows, :]

    def block(i, carry):
        cols = pl.ds(pl.multiple_of(i * width, width), width)
        re, im = e_ref[0, :, cols], n_ref[0, :, cols]
        re, im = turn_norm * (re + coriolis * im), turn_norm * (im - coriolis * re)
        for step in range(1, steps):
            re, im = re + e_ref[step, :, cols], im + n_ref[step, :, cols]
            re, im = turn_norm * (re + coriolis * im), turn_norm * (im - coriolis * re)
        out_ref[0, :, cols] = re
        out_ref[1, :, cols] = im
        return carry

    lax.fori_loop(0, total // width, block, 0)


def sublane(x):
    return lax.broadcasted_iota(jnp.int32, x.shape, 0)


def pack_rows(tiles, first):
    out = []
    for t in range(-(-3 * len(tiles) // 8)):
        packed = None
        for k, tile in enumerate(tiles):
            at = 3 * k - 8 * t
            if -3 < at < 8:
                moved = pltpu.roll(tile, (at - first) % 8, 0) if (at - first) % 8 else tile
                packed = moved if packed is None else jnp.where(sublane(tile) >= at, moved, packed)
        out.append(packed)
    return out


def unpack_rows(load, k, first):
    t = 3 * k // 8
    tile = load(t)
    at = 3 * k - 8 * t
    out = pltpu.roll(tile, (first - at) % 8, 0) if (first - at) % 8 else tile
    if at > 5:
        other = pltpu.roll(load(t + 1), (first - at) % 8, 0) if (first - at) % 8 else load(t + 1)
        out = jnp.where(sublane(tile) >= first + 8 - at, other, out)
    return out


def halo_tile(after, before, k):
    a, b = unpack_rows(after, k, 0), unpack_rows(before, k, 5)
    return jnp.where(sublane(a) < 4, a, b)


def source_kernel(
    h_ref, e_ref, n_ref, before_ref, after_ref, src_ref, prev_ref, next_ref, *states, parts, width
):
    steps, rows, total = h_ref.shape

    def block(start, edge, edge_cols, inner, inner_cols):
        cols = pl.ds(start, width)
        row = lax.broadcasted_iota(jnp.int32, (rows, width), 0)
        first, last = row == 0, row == rows - 1
        low = low_half((8, width))

        def slopes(ref, step, at):
            x = wide(lambda c: ref[step, :, c], start, width, total)
            mid = core(x)
            line = pl.ds(at + step, 1)
            up = jnp.where(last, after_ref[line, cols], next_row(mid))
            down = jnp.where(first, before_ref[line, cols], previous_row(mid))
            return dx(x), 0.5 * (up - down)

        p = jnp.zeros((rows, width), jnp.float32)
        state = [p] * 6
        edges = []
        h_last = None
        for step in range(steps):
            h = h_ref[step, :, cols]
            e_x, e_y = slopes(e_ref, step, 0)
            n_x, n_y = slopes(n_ref, step, steps)
            p = p + (coriolis * h - mean_depth * (n_x - e_y))
            change = h if h_last is None else h - h_last
            src = (change - mean_depth * (e_x + n_y)) + coriolis * p
            h_last = h
            src_ref[step, :, cols] = src
            top, bottom = src[:8], src[8:]
            edges.append(jnp.where(low, top, bottom))
            state = advance(src, state)
        for ref, first in ((prev_ref, 0), (next_ref, 5)):
            for t, tile in enumerate(pack_rows(edges, first)):
                ref[t, :, cols] = tile
        state[0] = state[0] - h_last
        for k, value in enumerate([p] + state):
            top, bottom = value[:8], value[8:]
            states[edge][k, :, edge_cols] = jnp.where(low, top, bottom)
            states[inner][k, :, inner_cols] = jnp.where(low, bottom, top)

    over_segments(parts, width, block)


def advance(source, state):
    out, x = [], source
    for k in range(3):
        u, r = state[2 * k], state[2 * k + 1]
        new = (x + u) * (1.0 / diagonal)
        out += [2.0 * new - r, new]
        x = wave_speed * new
    return out


def mix_kernel(*refs, weights, width):
    *args, out_ref = refs
    count, _, total = out_ref.shape
    me = lax.axis_index("tm")

    def run(matrices):
        def block(i, carry):
            cols = pl.ds(pl.multiple_of(i * width, width), width)
            sums = [None] * count
            for ref, matrix in zip(args, matrices):
                if matrix is None:
                    continue
                fields = [ref[k, :, cols] for k in range(count)]
                for k in range(count):
                    for j in range(count):
                        weight = float(np.float32(matrix[k, j]))
                        if weight != 0.0:
                            term = fields[j] if weight == 1.0 else weight * fields[j]
                            sums[k] = term if sums[k] is None else sums[k] + term
            for k in range(count):
                out_ref[k, :, cols] = sums[k]
            return carry

        lax.fori_loop(0, total // width, block, 0)

    for b, matrices in enumerate(weights):
        if matrices is not None:
            pl.when(me == b)(functools.partial(run, matrices))


def segments(total, bounds):
    cuts = sorted({x % total for x in bounds} | {total})

    def place(x):
        chunk = max(c for c in range(len(bounds) - 1) if bounds[c] <= x)
        return chunk, x - bounds[chunk]

    return [(a, b - a, place(a), place(total + a)) for a, b in zip(cuts[:-1], cuts[1:])]


def over_segments(parts, width, body):
    for start, size, (edge, edge_at), (inner, inner_at) in parts:

        def block(i, carry):
            at = [pl.multiple_of(x + i * width, LANES) for x in (start, edge_at, inner_at)]
            body(at[0], edge, pl.ds(at[1], width), inner, pl.ds(at[2], width))
            return carry

        lax.fori_loop(0, size // width, block, 0)


def pack_kernel(*refs, parts, width):
    *states, prev_ref, next_ref = refs

    def block(start, edge, there, *_):
        cols = pl.ds(start, width)
        tiles = [states[edge][k, :, there] for k in range(7)]
        for ref, first in ((prev_ref, 0), (next_ref, 5)):
            for t, tile in enumerate(pack_rows(tiles, first)):
                ref[t, :, cols] = tile

    over_segments(parts, width, block)


def pack_turn_kernel(src_prev_ref, src_next_ref, phi_ref, prev_ref, next_ref):
    count, _, total = src_prev_ref.shape
    low = low_half((8, total))
    prev_ref[:count] = src_prev_ref[...]
    next_ref[:count] = src_next_ref[...]
    prev_ref[count] = jnp.where(low, phi_ref[0, :8], pltpu.roll(phi_ref[1, :8], 4, 0))
    next_ref[count] = jnp.where(low, pltpu.roll(phi_ref[1, 8:], 4, 0), phi_ref[0, 8:])


def final_kernel(*refs, parts, width):
    count = 1 + max(inner for _, _, _, (inner, _) in parts)
    states, refs = refs[:count], refs[count:]
    (
        phi_ref, s_after_ref, s_before_ref, src_ref, src_after_ref, src_before_ref, e_hbm, n_hbm,
        h_out, e_out, n_out, r1, r2, r3, ring, e_ref, n_ref, u_ref, v_ref, sems,
    ) = refs
    steps, rows, total = src_ref.shape
    copies_in = [
        pltpu.make_async_copy(e_hbm, e_ref, sems.at[0]),
        pltpu.make_async_copy(n_hbm, n_ref, sems.at[1]),
    ]
    for copy in copies_in:
        copy.start()
    lines = [np.asarray(line) for line in start_rows()]

    def filters(start, edge_at, edge_cols, inner_at, inner_cols):
        cols = pl.ds(start, width)
        low = low_half((8, width))
        fields = []
        for k in range(7):
            edge, inner = states[edge_at][k, :, edge_cols], states[inner_at][k, :, inner_cols]
            halo = halo_tile(lambda t: s_after_ref[t, :, cols], lambda t: s_before_ref[t, :, cols], k)
            fields.append(
                jnp.concatenate([jnp.where(low, edge, inner), jnp.where(low, inner, edge), halo], 0)
            )
        turned_tile = src_after_ref.shape[0] - 1
        a, b = src_after_ref[turned_tile, :, cols], src_before_ref[turned_tile, :, cols]
        ring[0, :, cols] = jnp.concatenate([phi_ref[0, :, cols], jnp.where(low, a, b)], 0)
        ring[1, :, cols] = jnp.concatenate(
            [phi_ref[1, :, cols], pltpu.roll(jnp.where(low, b, a), 4, 0)], 0
        )
        for planes, line in ((r1, lines[0]), (r2, lines[1]), (r3, lines[2])):
            for part, weights in ((0, np.real(line)), (1, np.imag(line))):
                value = None
                for j in range(7):
                    if weights[j] != 0.0:
                        term = float(weights[j]) * fields[j]
                        value = term if value is None else value + term
                planes[steps + part, :, cols] = value
        turned = coriolis * fields[0]
        state = fields[1:]
        for step in range(steps):
            halo = halo_tile(lambda t: src_after_ref[t, :, cols], lambda t: src_before_ref[t, :, cols], step)
            source = jnp.concatenate([src_ref[step, :, cols], halo], 0) + turned
            state = advance(source, state)
            r1[step, :, cols] = state[1]
            r2[step, :, cols] = state[3]
            r3[step, :, cols] = state[5]

    over_segments(parts, width, filters)

    def row_dx(x):
        return 0.5 * (pltpu.roll(x, total - 1, 1) - pltpu.roll(x, 1, 1))

    def row_neighbours(x):
        return (next_row(x) + previous_row(x)) + (pltpu.roll(x, total - 1, 1) + pltpu.roll(x, 1, 1))

    re, im = ring[0], ring[1]
    chi = (row_dx(re) + dy(im), row_dx(im) - dy(re))
    share = mean_depth / (4.0 * wave_speed)
    for planes, part_share in ((r1, share), (r2, share / 4.0), (r3, share / 16.0)):
        for part in range(2):
            planes[steps + part] = planes[steps + part] - part_share * chi[part]
    for low_planes, high_planes in ((r2, r3), (r1, r2)):
        for k in range(steps + 2):
            low_planes[k] = low_planes[k] + row_neighbours(high_planes[k])
    height_copy = pltpu.make_async_copy(r1.at[pl.ds(0, steps), pl.ds(0, rows)], h_out, sems.at[2])
    height_copy.start()
    for copy in copies_in:
        copy.wait()

    def slopes(k):
        x = r1[k]
        return row_dx(x[:rows]), dy(x)[:rows]

    re_x, re_y = slopes(steps)
    im_x, im_y = slopes(steps + 1)
    u = ring[0, :rows] - gravity * (re_x - im_y)
    v = ring[1, :rows] - gravity * (im_x + re_y)
    copies_out = [height_copy]
    for step in range(steps):
        eta_x, eta_y = slopes(step)
        re = u + (e_ref[step] - gravity * eta_x)
        im = v + (n_ref[step] - gravity * eta_y)
        u, v = turn_norm * (re + coriolis * im), turn_norm * (im - coriolis * re)
        u_ref[step] = u
        v_ref[step] = v
        for ref, out, sem in ((u_ref, e_out, 3 + 2 * step), (v_ref, n_out, 4 + 2 * step)):
            copies_out.append(pltpu.make_async_copy(ref.at[step], out.at[step], sems.at[sem]))
            copies_out[-1].start()
    for copy in copies_out:
        copy.wait()


VMEM = pl.BlockSpec(memory_space=pltpu.VMEM)
ANY = pl.BlockSpec(memory_space=pl.ANY)


def f32(*shape):
    return jax.ShapeDtypeStruct(shape, jnp.float32)


def call(kernel, args, outs, name, in_specs=None, limit=16, scratch=(), out_specs=None, after=()):
    count = len(args)

    def run(*refs):
        kernel(*refs[:count], *refs[count + len(after) :])

    return pl.pallas_call(
        run,
        out_shape=outs,
        in_specs=(in_specs or [VMEM] * count) + [ANY] * len(after),
        out_specs=out_specs or [VMEM] * len(outs),
        scratch_shapes=scratch,
        compiler_params=pltpu.CompilerParams(vmem_limit_bytes=limit * MIB),
        cost_estimate=pl.CostEstimate(flops=COST, bytes_accessed=1000, transcendentals=0),
        name=name,
    )(*args, *after)


def shifts(axis):
    count = lax.axis_size(axis)
    forward = [(i, (i + 1) % count) for i in range(count)]
    return forward, [(t, s) for s, t in forward]


CHUNKS = 4
LAG = 1.01
FIN = 0.0
SINCE = 7
COST = 2 * 10**9


def body(h, e, n):
    steps, rows, total = h.shape
    parts = lax.axis_size("tm")
    unit = 256 if total % 256 == 0 and 2 * total >= 256 * CHUNKS else LANES
    bounds = [-(-2 * total // unit * i // CHUNKS) * unit for i in range(CHUNKS + 1)]
    places = segments(total, bounds)
    fields_block, turn_block = transitions(steps)
    forward, backward = shifts("space")

    def hop(x, k):
        return lax.ppermute(x, "tm", [(k - 1, k), (parts - k, parts - 1 - k)])

    def mix(args, weights, name, after):
        kernel = functools.partial(mix_kernel, weights=weights, width=unit)
        return call(kernel, args, [f32(*args[0].shape)], name, limit=8, after=after)[0]

    line = f32(2 * steps, total)
    whole = pltpu.VMEM((steps, rows, total), jnp.float32)
    phi, first_rows, last_rows = call(
        functools.partial(turn_kernel, width=unit), [e, n], [f32(2, rows, total), line, line], "turn",
        [ANY] * 2, scratch=[whole, whole, pltpu.SemaphoreType.DMA((steps,))],
    )
    before = lax.ppermute(last_rows, "space", forward)
    after = lax.ppermute(first_rows, "space", backward)
    src_tiles = -(-3 * steps // 8)
    pack = f32(src_tiles, 8, total)
    src, src_prev, src_next, *states = call(
        functools.partial(source_kernel, parts=places, width=2 * unit),
        [h, e, n, before, after],
        [f32(steps, rows, total), pack, pack] + [f32(7, 8, b - a) for a, b in zip(bounds[:-1], bounds[1:])],
        "source",
    )

    chunks = [(phi, turn_block)] + [(x, fields_block) for x in states]
    message = [own for own, _ in chunks]
    brought = [[] for _ in chunks]
    done = [None] * len(chunks)
    last_edge = 1 + max(edge for _, _, (edge, _), _ in places)
    latest, packs = states[0], None
    since = packs_sent = 0
    order = [(j, k) for j in range(len(chunks)) for k in range(1, parts)]
    for j, k in sorted(order, key=lambda jk: jk[0] + (jk[1] - 1) * LAG + FIN * (jk[1] == parts - 1)):
        own, block = chunks[j]
        deps = [latest]
        since += packs_sent
        if since == SINCE:
            deps += [src_after, src_before]
        brought[j].append(hop(message[j], k))
        if k < parts - 1:
            message[j] = mix([brought[j][-1], own], message_weights(block, parts, k), f"message_{j}_{k}", deps)
            latest = message[j]
        if k == max(parts - 2, 1):
            weights = [[arrival_weight(block, parts, b, i) for i in range(k + 1)] for b in range(parts)]
            done[j] = mix([own] + brought[j], weights, f"settle_{j}", [latest])
        if k == parts - 1 and k > 1:
            weights = [[np.eye(len(block)), arrival_weight(block, parts, b, k)] for b in range(parts)]
            done[j] = mix([done[j], brought[j][-1]], weights, f"finish_{j}", deps)
            latest = done[j]
        if k == parts - 1 and j == 0:
            src_prev, src_next = call(
                pack_turn_kernel, [src_prev, src_next, done[0]], [f32(src_tiles + 1, 8, total)] * 2, "pack_turn",
                limit=8,
            )
            src_after = lax.ppermute(src_prev, "space", backward)
            src_before = lax.ppermute(src_next, "space", forward)
            latest, packs_sent = src_prev, 1
        if k == parts - 1 and j == last_edge:
            packs = call(
                functools.partial(pack_kernel, parts=places, width=unit),
                done[1 : 1 + last_edge], [f32(3, 8, total)] * 2, "pack", limit=8,
            )
            latest = packs[0]
    to_prev, to_next = packs
    s_after = lax.ppermute(to_prev, "space", backward)
    s_before = lax.ppermute(to_next, "space", forward)

    planes = pltpu.VMEM((steps + 2, rows + 8, total), jnp.float32)
    return tuple(
        call(
            functools.partial(final_kernel, parts=places, width=unit),
            done[1:] + [done[0], s_after, s_before, src, src_after, src_before, e, n],
            [f32(steps, rows, total)] * 3,
            "final",
            [VMEM] * (CHUNKS + 6) + [ANY] * 2,
            24,
            [planes, planes, planes, pltpu.VMEM((2, rows + 8, total), jnp.float32)]
            + [whole] * 4
            + [pltpu.SemaphoreType.DMA((3 + 2 * steps,))],
            [ANY] * 3,
        )
    )


def solution(mesh):
    specs = (P("tm", "space", None),) * 3
    return jax.shard_map(body, mesh=mesh, in_specs=specs, out_specs=specs, check_vma=False)
```

```python
import functools
import math

import jax
import jax.numpy as jnp
import numpy as np
from jax import lax
from jax.experimental import pallas as pl
from jax.experimental.pallas import tpu as pltpu
from jax.sharding import PartitionSpec as P

alpha_window = 0.1
gravity = 1.0
mean_depth = 0.25
coriolis = 0.3
wave_speed = gravity * mean_depth
diagonal = 1.0 + coriolis * coriolis + 4.0 * wave_speed
turn_norm = 1.0 / (1.0 + coriolis * coriolis)
LANES = 128
MIB = 1 << 20


def step_matrix():
    m = np.zeros((7, 7))
    m[0, 0] = 1.0
    source = np.zeros(7)
    source[0] = coriolis
    for k in range(3):
        u, r = 1 + 2 * k, 2 + 2 * k
        new = source.copy()
        new[u] += 1.0
        new = new / diagonal
        m[r] = new
        m[u] = 2.0 * new
        m[u, r] -= 1.0
        source = wave_speed * new
    return m


def turn_matrix(value):
    return np.array([[np.real(value), -np.imag(value)], [np.imag(value), np.real(value)]])


def transitions(steps_local):
    spin = (1.0 / (1.0 + 1j * coriolis)) ** steps_local
    return np.linalg.matrix_power(step_matrix(), steps_local), turn_matrix(spin)


def message_weights(block, parts, hop):
    eye, power = np.eye(len(block)), np.linalg.matrix_power
    weights = [None] * parts
    weights[hop] = [block, eye]
    weights[parts - 1 - hop] = [eye, power(block, hop)]
    return weights


def arrival_weight(block, parts, b, hop):
    power = np.linalg.matrix_power
    closure = np.linalg.inv(np.eye(len(block)) - alpha_window * power(block, parts))
    if hop == 0:
        return alpha_window * closure @ power(block, parts - 1)
    if hop == b:
        return closure
    if hop == parts - 1 - b:
        return alpha_window * closure @ power(block, b)
    return None


def start_rows():
    one = step_matrix()
    inverse = np.linalg.inv((1.0 + 1j * coriolis) * one - np.eye(7))
    return [one[2 + 2 * k] @ inverse for k in range(3)]


def low_half(shape):
    return lax.broadcasted_iota(jnp.int32, shape, len(shape) - 2) < 4


def wide(load, start, width, total):
    left = pl.multiple_of(lax.rem(start + (total - LANES), total), LANES)
    right = pl.multiple_of(lax.rem(start + width, total), LANES)
    return jnp.concatenate(
        [load(pl.ds(left, LANES)), load(pl.ds(start, width)), load(pl.ds(right, LANES))], axis=-1
    )


def core(x):
    return x[:, LANES : x.shape[1] - LANES]


def next_column(x):
    return core(pltpu.roll(x, x.shape[1] - 1, 1))


def previous_column(x):
    return core(pltpu.roll(x, 1, 1))


def next_row(x):
    return pltpu.roll(x, x.shape[0] - 1, 0)


def previous_row(x):
    return pltpu.roll(x, 1, 0)


def dx(x):
    return 0.5 * (next_column(x) - previous_column(x))


def dy(x):
    return 0.5 * (next_row(x) - previous_row(x))


def turn_kernel(e_hbm, n_hbm, out_ref, prev_ref, next_ref, e_ref, n_ref, sems, *, width):
    steps, rows, total = e_ref.shape
    copies = []
    for step in range(0, steps, 2):
        part = pl.ds(step, 2)
        copies.append(pltpu.make_async_copy(e_hbm.at[part], e_ref.at[part], sems.at[step]))
        copies.append(pltpu.make_async_copy(n_hbm.at[part], n_ref.at[part], sems.at[step + 1]))
    for copy in copies:
        copy.start()
    for copy in copies:
        copy.wait()
    for step in range(steps):
        for ref, at in ((e_ref, step), (n_ref, steps + step)):
            prev_ref[at : at + 1, :] = ref[step, 0:1, :]
            next_ref[at : at + 1, :] = ref[step, rows - 1 : rows, :]

    def block(i, carry):
        cols = pl.ds(pl.multiple_of(i * width, width), width)
        re, im = e_ref[0, :, cols], n_ref[0, :, cols]
        re, im = turn_norm * (re + coriolis * im), turn_norm * (im - coriolis * re)
        for step in range(1, steps):
            re, im = re + e_ref[step, :, cols], im + n_ref[step, :, cols]
            re, im = turn_norm * (re + coriolis * im), turn_norm * (im - coriolis * re)
        out_ref[0, :, cols] = re
        out_ref[1, :, cols] = im
        return carry

    lax.fori_loop(0, total // width, block, 0)


def sublane(x):
    return lax.broadcasted_iota(jnp.int32, x.shape, 0)


def pack_rows(tiles, first):
    out = []
    for t in range(-(-3 * len(tiles) // 8)):
        packed = None
        for k, tile in enumerate(tiles):
            at = 3 * k - 8 * t
            if -3 < at < 8:
                moved = pltpu.roll(tile, (at - first) % 8, 0) if (at - first) % 8 else tile
                packed = moved if packed is None else jnp.where(sublane(tile) >= at, moved, packed)
        out.append(packed)
    return out


def unpack_rows(load, k, first):
    t = 3 * k // 8
    tile = load(t)
    at = 3 * k - 8 * t
    out = pltpu.roll(tile, (first - at) % 8, 0) if (first - at) % 8 else tile
    if at > 5:
        other = pltpu.roll(load(t + 1), (first - at) % 8, 0) if (first - at) % 8 else load(t + 1)
        out = jnp.where(sublane(tile) >= first + 8 - at, other, out)
    return out


def halo_tile(after, before, k):
    a, b = unpack_rows(after, k, 0), unpack_rows(before, k, 5)
    return jnp.where(sublane(a) < 4, a, b)


def source_kernel(
    h_ref, e_ref, n_ref, before_ref, after_ref, src_ref, prev_ref, next_ref, *states, parts, width
):
    steps, rows, total = h_ref.shape

    def block(start, edge, edge_cols, inner, inner_cols):
        cols = pl.ds(start, width)
        row = lax.broadcasted_iota(jnp.int32, (rows, width), 0)
        first, last = row == 0, row == rows - 1
        low = low_half((8, width))

        def slopes(ref, step, at):
            x = wide(lambda c: ref[step, :, c], start, width, total)
            mid = core(x)
            line = pl.ds(at + step, 1)
            up = jnp.where(last, after_ref[line, cols], next_row(mid))
            down = jnp.where(first, before_ref[line, cols], previous_row(mid))
            return dx(x), 0.5 * (up - down)

        p = jnp.zeros((rows, width), jnp.float32)
        state = [p] * 6
        edges = []
        h_last = None
        for step in range(steps):
            h = h_ref[step, :, cols]
            e_x, e_y = slopes(e_ref, step, 0)
            n_x, n_y = slopes(n_ref, step, steps)
            p = p + (coriolis * h - mean_depth * (n_x - e_y))
            change = h if h_last is None else h - h_last
            src = (change - mean_depth * (e_x + n_y)) + coriolis * p
            h_last = h
            src_ref[step, :, cols] = src
            top, bottom = src[:8], src[8:]
            edges.append(jnp.where(low, top, bottom))
            state = advance(src, state)
        for ref, first in ((prev_ref, 0), (next_ref, 5)):
            for t, tile in enumerate(pack_rows(edges, first)):
                ref[t, :, cols] = tile
        state[0] = state[0] - h_last
        for k, value in enumerate([p] + state):
            top, bottom = value[:8], value[8:]
            states[edge][k, :, edge_cols] = jnp.where(low, top, bottom)
            states[inner][k, :, inner_cols] = jnp.where(low, bottom, top)

    over_segments(parts, width, block)


def advance(source, state):
    out, x = [], source
    for k in range(3):
        u, r = state[2 * k], state[2 * k + 1]
        new = (x + u) * (1.0 / diagonal)
        out += [2.0 * new - r, new]
        x = wave_speed * new
    return out


def mix_kernel(*refs, weights, width):
    *args, out_ref = refs
    count, _, total = out_ref.shape
    me = lax.axis_index("tm")

    def run(matrices):
        def block(i, carry):
            cols = pl.ds(pl.multiple_of(i * width, width), width)
            sums = [None] * count
            for ref, matrix in zip(args, matrices):
                if matrix is None:
                    continue
                fields = [ref[k, :, cols] for k in range(count)]
                for k in range(count):
                    for j in range(count):
                        weight = float(np.float32(matrix[k, j]))
                        if weight != 0.0:
                            term = fields[j] if weight == 1.0 else weight * fields[j]
                            sums[k] = term if sums[k] is None else sums[k] + term
            for k in range(count):
                out_ref[k, :, cols] = sums[k]
            return carry

        lax.fori_loop(0, total // width, block, 0)

    for b, matrices in enumerate(weights):
        if matrices is not None:
            pl.when(me == b)(functools.partial(run, matrices))


def segments(total, bounds):
    cuts = sorted({x % total for x in bounds} | {total})

    def place(x):
        chunk = max(c for c in range(len(bounds) - 1) if bounds[c] <= x)
        return chunk, x - bounds[chunk]

    return [(a, b - a, place(a), place(total + a)) for a, b in zip(cuts[:-1], cuts[1:])]


def over_segments(parts, width, body):
    for start, size, (edge, edge_at), (inner, inner_at) in parts:

        def block(i, carry):
            at = [pl.multiple_of(x + i * width, LANES) for x in (start, edge_at, inner_at)]
            body(at[0], edge, pl.ds(at[1], width), inner, pl.ds(at[2], width))
            return carry

        lax.fori_loop(0, size // width, block, 0)


def pack_kernel(*refs, parts, width):
    *states, prev_ref, next_ref = refs

    def block(start, edge, there, *_):
        cols = pl.ds(start, width)
        tiles = [states[edge][k, :, there] for k in range(7)]
        for ref, first in ((prev_ref, 0), (next_ref, 5)):
            for t, tile in enumerate(pack_rows(tiles, first)):
                ref[t, :, cols] = tile

    over_segments(parts, width, block)


def pack_turn_kernel(src_prev_ref, src_next_ref, phi_ref, prev_ref, next_ref):
    count, _, total = src_prev_ref.shape
    low = low_half((8, total))
    prev_ref[:count] = src_prev_ref[...]
    next_ref[:count] = src_next_ref[...]
    prev_ref[count] = jnp.where(low, phi_ref[0, :8], pltpu.roll(phi_ref[1, :8], 4, 0))
    next_ref[count] = jnp.where(low, pltpu.roll(phi_ref[1, 8:], 4, 0), phi_ref[0, 8:])


def final_kernel(*refs, parts, width):
    count = 1 + max(inner for _, _, _, (inner, _) in parts)
    states, refs = refs[:count], refs[count:]
    (
        phi_ref, s_after_ref, s_before_ref, src_ref, src_after_ref, src_before_ref, e_hbm, n_hbm,
        h_out, e_out, n_out, r1, r2, r3, ring, e_ref, n_ref, u_ref, v_ref, sems,
    ) = refs
    steps, rows, total = src_ref.shape
    copies_in = [
        pltpu.make_async_copy(e_hbm, e_ref, sems.at[0]),
        pltpu.make_async_copy(n_hbm, n_ref, sems.at[1]),
    ]
    for copy in copies_in:
        copy.start()
    lines = [np.asarray(line) for line in start_rows()]

    def filters(start, edge_at, edge_cols, inner_at, inner_cols):
        cols = pl.ds(start, width)
        low = low_half((8, width))
        fields = []
        for k in range(7):
            edge, inner = states[edge_at][k, :, edge_cols], states[inner_at][k, :, inner_cols]
            halo = halo_tile(lambda t: s_after_ref[t, :, cols], lambda t: s_before_ref[t, :, cols], k)
            fields.append(
                jnp.concatenate([jnp.where(low, edge, inner), jnp.where(low, inner, edge), halo], 0)
            )
        turned_tile = src_after_ref.shape[0] - 1
        a, b = src_after_ref[turned_tile, :, cols], src_before_ref[turned_tile, :, cols]
        ring[0, :, cols] = jnp.concatenate([phi_ref[0, :, cols], jnp.where(low, a, b)], 0)
        ring[1, :, cols] = jnp.concatenate(
            [phi_ref[1, :, cols], pltpu.roll(jnp.where(low, b, a), 4, 0)], 0
        )
        for planes, line in ((r1, lines[0]), (r2, lines[1]), (r3, lines[2])):
            for part, weights in ((0, np.real(line)), (1, np.imag(line))):
                value = None
                for j in range(7):
                    if weights[j] != 0.0:
                        term = float(weights[j]) * fields[j]
                        value = term if value is None else value + term
                planes[steps + part, :, cols] = value
        turned = coriolis * fields[0]
        state = fields[1:]
        for step in range(steps):
            halo = halo_tile(lambda t: src_after_ref[t, :, cols], lambda t: src_before_ref[t, :, cols], step)
            source = jnp.concatenate([src_ref[step, :, cols], halo], 0) + turned
            state = advance(source, state)
            r1[step, :, cols] = state[1]
            r2[step, :, cols] = state[3]
            r3[step, :, cols] = state[5]

    over_segments(parts, width, filters)

    def row_dx(x):
        return 0.5 * (pltpu.roll(x, total - 1, 1) - pltpu.roll(x, 1, 1))

    def row_neighbours(x):
        return (next_row(x) + previous_row(x)) + (pltpu.roll(x, total - 1, 1) + pltpu.roll(x, 1, 1))

    re, im = ring[0], ring[1]
    chi = (row_dx(re) + dy(im), row_dx(im) - dy(re))
    share = mean_depth / (4.0 * wave_speed)
    for planes, part_share in ((r1, share), (r2, share / 4.0), (r3, share / 16.0)):
        for part in range(2):
            planes[steps + part] = planes[steps + part] - part_share * chi[part]
    for low_planes, high_planes in ((r2, r3), (r1, r2)):
        for k in range(steps + 2):
            low_planes[k] = low_planes[k] + row_neighbours(high_planes[k])
    height_copy = pltpu.make_async_copy(r1.at[pl.ds(0, steps), pl.ds(0, rows)], h_out, sems.at[2])
    height_copy.start()
    for copy in copies_in:
        copy.wait()

    def slopes(k):
        x = r1[k]
        return row_dx(x[:rows]), dy(x)[:rows]

    re_x, re_y = slopes(steps)
    im_x, im_y = slopes(steps + 1)
    u = ring[0, :rows] - gravity * (re_x - im_y)
    v = ring[1, :rows] - gravity * (im_x + re_y)
    copies_out = [height_copy]
    for step in range(steps):
        eta_x, eta_y = slopes(step)
        re = u + (e_ref[step] - gravity * eta_x)
        im = v + (n_ref[step] - gravity * eta_y)
        u, v = turn_norm * (re + coriolis * im), turn_norm * (im - coriolis * re)
        u_ref[step] = u
        v_ref[step] = v
        for ref, out, sem in ((u_ref, e_out, 3 + 2 * step), (v_ref, n_out, 4 + 2 * step)):
            copies_out.append(pltpu.make_async_copy(ref.at[step], out.at[step], sems.at[sem]))
            copies_out[-1].start()
    for copy in copies_out:
        copy.wait()


VMEM = pl.BlockSpec(memory_space=pltpu.VMEM)
ANY = pl.BlockSpec(memory_space=pl.ANY)


def f32(*shape):
    return jax.ShapeDtypeStruct(shape, jnp.float32)


def call(kernel, args, outs, name, in_specs=None, limit=16, scratch=(), out_specs=None, after=(), flops=None):
    count = len(args)

    def run(*refs):
        kernel(*refs[:count], *refs[count + len(after) :])

    return pl.pallas_call(
        run,
        out_shape=outs,
        in_specs=(in_specs or [VMEM] * count) + [ANY] * len(after),
        out_specs=out_specs or [VMEM] * len(outs),
        scratch_shapes=scratch,
        compiler_params=pltpu.CompilerParams(vmem_limit_bytes=limit * MIB),
        cost_estimate=pl.CostEstimate(flops=COST if flops is None else flops, bytes_accessed=1000, transcendentals=0),
        name=name,
    )(*args, *after)


def shifts(axis):
    count = lax.axis_size(axis)
    forward = [(i, (i + 1) % count) for i in range(count)]
    return forward, [(t, s) for s, t in forward]


CHUNKS = 4
LAG = 1.01
SETTLE = 0
FINISH = 0
SINCE = 8
COST = 25 * 10**8


def body(h, e, n):
    steps, rows, total = h.shape
    parts = lax.axis_size("tm")
    unit = 256 if total % 256 == 0 and 2 * total >= 256 * CHUNKS else LANES
    bounds = [-(-2 * total // unit * i // CHUNKS) * unit for i in range(CHUNKS + 1)]
    places = segments(total, bounds)
    span = math.gcd(4 * unit, *(size for _, size, _, _ in places))
    fields_block, turn_block = transitions(steps)
    forward, backward = shifts("space")

    def hop(x, k):
        return lax.ppermute(x, "tm", [(k - 1, k), (parts - k, parts - 1 - k)])

    def mix(args, weights, name, after, flops=None):
        kernel = functools.partial(mix_kernel, weights=weights, width=unit)
        return call(kernel, args, [f32(*args[0].shape)], name, limit=8, after=after, flops=flops)[0]

    line = f32(2 * steps, total)
    whole = pltpu.VMEM((steps, rows, total), jnp.float32)
    phi, first_rows, last_rows = call(
        functools.partial(turn_kernel, width=unit), [e, n], [f32(2, rows, total), line, line], "turn",
        [ANY] * 2, scratch=[whole, whole, pltpu.SemaphoreType.DMA((steps,))],
    )
    before = lax.ppermute(last_rows, "space", forward)
    after = lax.ppermute(first_rows, "space", backward)
    src_tiles = -(-3 * steps // 8)
    pack = f32(src_tiles, 8, total)
    src, src_prev, src_next, *states = call(
        functools.partial(source_kernel, parts=places, width=min(span, 2 * unit)),
        [h, e, n, before, after],
        [f32(steps, rows, total), pack, pack] + [f32(7, 8, b - a) for a, b in zip(bounds[:-1], bounds[1:])],
        "source",
    )

    chunks = [(phi, turn_block)] + [(x, fields_block) for x in states]
    message = [own for own, _ in chunks]
    brought = [[] for _ in chunks]
    done = [None] * len(chunks)
    last_edge = 1 + max(edge for _, _, (edge, _), _ in places)
    latest, packs = states[0], None
    since = packs_sent = 0
    order = [(j, k) for j in range(len(chunks)) for k in range(1, parts)]
    for j, k in sorted(order, key=lambda jk: jk[0] + (jk[1] - 1) * LAG):
        own, block = chunks[j]
        deps = [latest]
        since += packs_sent
        if since == SINCE:
            deps += [src_after, src_before]
        brought[j].append(hop(message[j], k))
        if k < parts - 1:
            message[j] = mix([brought[j][-1], own], message_weights(block, parts, k), f"message_{j}_{k}", deps)
            latest = message[j]
        if k == max(parts - 2, 1):
            weights = [[arrival_weight(block, parts, b, i) for i in range(k + 1)] for b in range(parts)]
            done[j] = mix([own] + brought[j], weights, f"settle_{j}", [latest], SETTLE)
        if k == parts - 1 and k > 1:
            weights = [[np.eye(len(block)), arrival_weight(block, parts, b, k)] for b in range(parts)]
            done[j] = mix([done[j], brought[j][-1]], weights, f"finish_{j}", deps, FINISH)
            latest = done[j]
        if k == parts - 1 and j == 0:
            src_prev, src_next = call(
                pack_turn_kernel, [src_prev, src_next, done[0]], [f32(src_tiles + 1, 8, total)] * 2, "pack_turn",
                limit=8,
            )
            src_after = lax.ppermute(src_prev, "space", backward)
            src_before = lax.ppermute(src_next, "space", forward)
            latest, packs_sent = src_prev, 1
        if k == parts - 1 and j == last_edge:
            packs = call(
                functools.partial(pack_kernel, parts=places, width=unit),
                done[1 : 1 + last_edge], [f32(3, 8, total)] * 2, "pack", limit=8,
            )
            latest = packs[0]
    to_prev, to_next = packs
    s_after = lax.ppermute(to_prev, "space", backward)
    s_before = lax.ppermute(to_next, "space", forward)

    planes = pltpu.VMEM((steps + 2, rows + 8, total), jnp.float32)
    return tuple(
        call(
            functools.partial(final_kernel, parts=places, width=span),
            done[1:] + [done[0], s_after, s_before, src, src_after, src_before, e, n],
            [f32(steps, rows, total)] * 3,
            "final",
            [VMEM] * (CHUNKS + 6) + [ANY] * 2,
            24,
            [planes, planes, planes, pltpu.VMEM((2, rows + 8, total), jnp.float32)]
            + [whole] * 4
            + [pltpu.SemaphoreType.DMA((3 + 2 * steps,))],
            [ANY] * 3,
        )
    )


def solution(mesh):
    specs = (P("tm", "space", None),) * 3
    return jax.shard_map(body, mesh=mesh, in_specs=specs, out_specs=specs, check_vma=False)
```
